128 devices in a mesh: ctx: 16 (over z_hi, x, core), tp: 8 (over y, z_lo).
Axes of the slice: x: 4, y: 4, z: 4 (z_hi: 2, z_lo: 2; z = z_hi * 2 + z_lo), core: 2. Of those that a mesh axis runs over, the one named last changes fastest.
Arguments:
- queries: bfloat16 [2048, 128, 128], P('ctx', 'tp'), may hold values from -8 to 8
- fresh_rotated_keys: bfloat16 [2048, 8, 128], P('ctx', 'tp'), may hold values from -4 to 4
- fresh_value_rows: bfloat16 [2048, 8, 128], P('ctx', 'tp'), may hold values from -5 to 5
- cache_keys: bfloat16 [16384, 8, 128], P('ctx', 'tp'), may hold values from -4 to 4
- prefix_value_rows: bfloat16 [16384, 8, 128], P('ctx', 'tp'), may hold values from -5 to 5
- cache_lengths: int32 [16], P('ctx'), may hold values from 256 to 1024, as said below
- new_segment: int32 [2048], replicated, may hold values from 0 to 3, never falling along the last dimension, each value on 1 to 1024 neighbouring positions
- out_weight: bfloat16 [16384, 16384], P('tp', 'ctx'), may hold values from -0.1875 to 0.1875
Outputs:
- attended: bfloat16 [2048, 128, 128], P('ctx', 'tp')
- mixed: bfloat16 [2048, 16384], P('tp', 'ctx')
The draws below stay inside these ranges and needn't reach their ends.
Inputs may be any that keep to these rules, and one draw needn't show every extreme that they name: `cache_lengths`: slots at or after the length of their index are unused; some index is full in every draw.
All inputs are finite; a program needn't handle non-finite values.
Results may differ from the reference program's by a relative error of at most 0.015.
Values may be sent and summed in bfloat16 or wider, within the bound.
No kernel may reach another device: no remote copies, remote signals or barrier semaphores. Data moves between devices by JAX's collectives and lax.ppermute only.
A program may use at most 64 MiB of HBM per device.

```python
import math
import jax
import jax.numpy as jnp
import numpy as np
from jax import lax

QUERY_HEADS = 128
KEY_VALUE_HEADS = 8
HEAD_SIZE = 128
D = 16384
QUERY_DEV = 128
CACHE_DEV = 1024
SEGS = 4
NEW_TOKEN_TOTAL = 2048
CACHE_SLOT_TOTAL = 16384
N_CTX = 16


def draw_queries(key, part):
    base_offset = jnp.clip(2.5 * jax.random.normal(jax.random.fold_in(key, 1), (NEW_TOKEN_TOTAL, QUERY_HEADS, HEAD_SIZE), jnp.float32), -8.0, 8.0)
    return base_offset.astype(jnp.bfloat16)


def draw_cache_keys(key, part):
    base_offset = jnp.clip(jax.random.normal(jax.random.fold_in(key, 5), (CACHE_SLOT_TOTAL, KEY_VALUE_HEADS, HEAD_SIZE), jnp.float32), -4.0, 4.0)
    return base_offset.astype(jnp.bfloat16)


def draw_cache_lengths(key, part):
    count = CACHE_SLOT_TOTAL // CACHE_DEV
    lengths = jax.random.randint(jax.random.fold_in(key, 2), (count,), CACHE_DEV // 4, CACHE_DEV + 1)
    picked = jax.random.randint(jax.random.fold_in(key, 3), (), 0, count)
    return lengths.at[picked].set(CACHE_DEV).astype(jnp.int32)


def shard_levels(own_key, extent, shards, smallest, top_value):
    factor_of = 1.0
    for position, shards_of in shards:
        draws = jax.random.uniform(jax.random.fold_in(jax.random.fold_in(own_key, 6), position), (shards_of,), jnp.float32, smallest / len(shards), top_value / len(shards))
        factor_of = factor_of * jnp.repeat(jnp.exp(draws), extent[position] // shards_of).reshape((-1,) + (1,) * (len(extent) - 1 - position))
    return factor_of


def split_up(amount, total, most, lean):
    portions = [(1 << 20) // math.isqrt(grade ** lean) + 1 for grade in range(2, amount + 1)]
    rest, holding = total - most - (amount - 1), [1] * (amount - 1)
    while rest > 0:
        candidates = [i for i in range(amount - 1) if holding[i] < most]
        mass, left = sum([portions[i] for i in candidates]), rest
        for i in candidates:
            more = min(most - holding[i], max(1, left * portions[i] // mass), rest)
            holding[i] = holding[i] + more
            rest = rest - more
    return np.array([most] + holding)


def ragged(own_key, count, total, most, lean):
    if count == 2:
        one = jax.random.randint(own_key, (), max(1, total - most), min(most, total - 1) + 1)
        return jnp.stack([one, total - one])
    sizes = jnp.asarray(split_up(count, total, most, lean), jnp.int32)
    pairs = (count - 1) // 2
    donor, receiver = sizes[1:1 + 2 * pairs:2], sizes[2:2 + 2 * pairs:2]
    room = jnp.minimum(donor - 1, most - receiver)
    moved = jax.random.randint(jax.random.fold_in(own_key, 1), (pairs,), 0, 1 << 20) % (room + 1)
    sizes = sizes.at[1:1 + 2 * pairs:2].set(donor - moved).at[2:2 + 2 * pairs:2].set(receiver + moved)
    return sizes[jax.random.permutation(jax.random.fold_in(own_key, 2), count)]


def scatter_about(rng, shape, deviation, limit, split=(), kind=jnp.bfloat16):
    factor_of = shard_levels(rng, shape, split, -0.22, 0.18) if split else 1.0
    entries = jax.random.normal(rng, shape, jnp.float32) * deviation * factor_of
    return jnp.minimum(jnp.maximum(entries, -limit), limit).astype(kind)


def setup_inputs(seed: int = 0) -> dict:
    key_of = jax.random.split(jax.random.key(seed), 9)
    return {
        "queries": draw_queries(jax.random.fold_in(key_of[8], 71), 0),
        "fresh_rotated_keys": scatter_about(key_of[1], (NEW_TOKEN_TOTAL, KEY_VALUE_HEADS, HEAD_SIZE), 1.0, 4.0, ((0, 16), (1, 8))),
        "fresh_value_rows": scatter_about(key_of[2], (NEW_TOKEN_TOTAL, KEY_VALUE_HEADS, HEAD_SIZE), 1.0, 5.0, ((0, 16), (1, 8))),
        "cache_keys": draw_cache_keys(jax.random.fold_in(key_of[8], 71), 0),
        "prefix_value_rows": scatter_about(key_of[4], (CACHE_SLOT_TOTAL, KEY_VALUE_HEADS, HEAD_SIZE), 1.0, 5.0, ((0, 16), (1, 8))),
        "cache_lengths": draw_cache_lengths(jax.random.fold_in(key_of[8], 71), 0),
        "new_segment": jnp.searchsorted(jnp.cumsum(ragged(key_of[6], SEGS, NEW_TOKEN_TOTAL, NEW_TOKEN_TOTAL // 2, 2)), jnp.arange(NEW_TOKEN_TOTAL), side="right").astype(jnp.int32),
        "out_weight": scatter_about(key_of[7], (QUERY_HEADS * HEAD_SIZE, D), (QUERY_HEADS * HEAD_SIZE // 16) ** -0.5, 0.1875, ((0, 8), (1, 16))),
    }


lowest_score_bound = -1e30


def attend(query_head, key_rows, value_rows, visible, scaling):
    scores = jnp.einsum("qrd,kd->qrk", query_head, key_rows) * scaling
    scores = jnp.where(visible[:, None, :], scores, lowest_score_bound)
    highest = jnp.max(scores, axis=-1)
    weights = jnp.exp(scores - highest[..., None])
    total = jnp.sum(weights, axis=-1)
    rounded = lax.optimization_barrier(weights.astype(jnp.bfloat16)).astype(jnp.float32)
    mixture = jnp.einsum("qrk,kd->qrd", rounded, value_rows) / total[..., None]
    return mixture.astype(jnp.bfloat16), highest + jnp.log(total)


def reference(queries, fresh_rotated_keys, fresh_value_rows, cache_keys, prefix_value_rows, cache_lengths, new_segment, out_weight):
    query_group = QUERY_HEADS // KEY_VALUE_HEADS
    scaling = HEAD_SIZE ** -0.5
    every_query_row = jnp.moveaxis(queries.astype(jnp.float32).reshape(NEW_TOKEN_TOTAL, KEY_VALUE_HEADS, query_group, HEAD_SIZE), 1, 0)
    positions = jnp.arange(NEW_TOKEN_TOTAL, dtype=jnp.int32)
    slots = jnp.arange(CACHE_DEV, dtype=jnp.int32)

    def shard_step(state, shard):
        run_max, run_sum, accum = state
        start_cache = (shard * CACHE_DEV).astype(jnp.int32)
        start_new = (shard * QUERY_DEV).astype(jnp.int32)
        key_rows = jnp.concatenate([lax.dynamic_slice_in_dim(cache_keys, start_cache, CACHE_DEV, 0), lax.dynamic_slice_in_dim(fresh_rotated_keys, start_new, QUERY_DEV, 0)], 0).astype(jnp.float32)
        value_rows = jnp.concatenate([lax.dynamic_slice_in_dim(prefix_value_rows, start_cache, CACHE_DEV, 0), lax.dynamic_slice_in_dim(fresh_value_rows, start_new, QUERY_DEV, 0)], 0).astype(jnp.float32)
        length = lax.dynamic_slice_in_dim(cache_lengths, shard, 1, 0)[0]
        key_pos = start_new + jnp.arange(QUERY_DEV, dtype=jnp.int32)
        key_seg = lax.dynamic_slice_in_dim(new_segment, start_new, QUERY_DEV, 0)
        cache_ok = jnp.broadcast_to((slots < length)[None, :], (NEW_TOKEN_TOTAL, CACHE_DEV))
        new_ok = (new_segment[:, None] == key_seg[None, :]) & (key_pos[None, :] <= positions[:, None])
        visible = jnp.concatenate([cache_ok, new_ok], 1)

        def per_head(inputs):
            query_head, key_head, value_head = inputs
            return attend(query_head, key_head, value_head, visible, scaling)

        mixtures, log_mass = lax.map(per_head, (every_query_row, jnp.moveaxis(key_rows, 1, 0), jnp.moveaxis(value_rows, 1, 0)))
        highest = jnp.maximum(run_max, log_mass)
        kept = jnp.exp(run_max - highest)
        fresh = jnp.exp(log_mass - highest)
        run_sum = run_sum * kept + fresh
        accum = accum * kept[..., None] + fresh[..., None] * mixtures.astype(jnp.float32)
        return (highest, run_sum, accum), None

    initial_state = (jnp.full((KEY_VALUE_HEADS, NEW_TOKEN_TOTAL, query_group), lowest_score_bound, jnp.float32), jnp.zeros((KEY_VALUE_HEADS, NEW_TOKEN_TOTAL, query_group), jnp.float32), jnp.zeros((KEY_VALUE_HEADS, NEW_TOKEN_TOTAL, query_group, HEAD_SIZE), jnp.float32))
    (run_max, run_sum, accum), _ = lax.scan(shard_step, initial_state, jnp.arange(N_CTX, dtype=jnp.int32))
    merged = accum / run_sum[..., None]
    attended = jnp.moveaxis(merged, 0, 1).reshape(NEW_TOKEN_TOTAL, QUERY_HEADS, HEAD_SIZE).astype(jnp.bfloat16)
    mixed = jnp.dot(attended.reshape(NEW_TOKEN_TOTAL, QUERY_HEADS * HEAD_SIZE), out_weight, preferred_element_type=jnp.float32).astype(jnp.bfloat16)
    return attended, mixed
```

```python
import functools
import math

import jax, jax.numpy as jnp
from jax import lax
from jax.experimental import pallas as pl
from jax.experimental.pallas import tpu as pltpu
from jax.sharding import Mesh, PartitionSpec as P

NEG = -1e30
CS = math.log2(math.e) / math.sqrt(128.0)
NT = (((1,), (1,)), ((), ()))

def attn_kernel(nsh, QB, SB, KB, scal, q_ref, *rest):
    k_refs, v_refs = rest[:nsh], rest[nsh:2*nsh]
    o_ref, lse_ref, lens, m, l, acc = rest[2*nsh:]
    i = pl.program_id(0)
    @pl.when(i == 0)
    def _():
        for s in range(nsh):
            t = k_refs[s][1152:1168, :].astype(jnp.float32)
            lens[s] = (jnp.max(t[0:8]) * 16.0 + jnp.max(t[8:16])).astype(jnp.int32)
    m[...] = jnp.full(m.shape, NEG, jnp.float32)
    l[...] = jnp.zeros(l.shape, jnp.float32)
    acc[...] = jnp.zeros(acc.shape, jnp.float32)
    nset = 2048 // QB
    base = scal[8 + i // nset] + (i % nset) * (QB // 16)
    lo_first = jnp.int32(0)
    for g in range(1, 4):
        lo_first = jnp.where(scal[g] <= base, scal[g], lo_first)

    def step(k, v, masks):
        n = k.shape[0] // 128
        for u in range(QB // SB):
            r = slice(u * SB, (u + 1) * SB)
            s = lax.dot_general(q_ref[r, :], k, NT, preferred_element_type=jnp.float32)
            if masks is not None:
                s = jnp.where(masks(u), s, NEG)
            mp = m[r, :]
            mn = jnp.maximum(mp, jnp.max(s, axis=1, keepdims=True))
            al = jnp.exp2((mp - mn) * CS)
            ps = [jnp.exp2((s[:, j*128:(j+1)*128] - mn) * CS) for j in range(n)]
            tot = ps[0]
            for p in ps[1:]:
                tot = tot + p
            l[r, :] = l[r, :] * al + tot
            pb = jnp.concatenate([p.astype(jnp.bfloat16) for p in ps], axis=1) if n > 1 else ps[0].astype(jnp.bfloat16)
            acc[r, :] = acc[r, :] * al + jnp.dot(pb, v, preferred_element_type=jnp.float32)
            m[r, :] = mn

    for s in range(nsh):
        k_ref, v_ref, n = k_refs[s], v_refs[s], lens[s]
        full = n // KB
        @pl.loop(0, full)
        def _(j):
            o = pl.multiple_of(j * KB, KB)
            step(k_ref[pl.ds(o, KB), :], v_ref[pl.ds(o, KB), :], None)
        @pl.when(full * KB < n)
        def _():
            o = pl.multiple_of(full * KB, KB)
            lane = lax.broadcasted_iota(jnp.int32, (SB, KB), 1) + o
            step(k_ref[pl.ds(o, KB), :], v_ref[pl.ds(o, KB), :], lambda u: lane < n)
        f = scal[4 + s]
        @pl.when((f <= base + (QB // 16 - 1)) & (f + 127 >= lo_first))
        def _():
            def mk(u):
                qp = base + u * (SB // 16) + lax.broadcasted_iota(jnp.int32, (SB, 128), 0) // 16
                lo = jnp.zeros((SB, 128), jnp.int32)
                for g in range(1, 4):
                    lo = jnp.where(scal[g] <= qp, scal[g], lo)
                kp = f + lax.broadcasted_iota(jnp.int32, (SB, 128), 1)
                return (kp <= qp) & (kp >= lo)
            step(k_ref[1024:1152, :], v_ref[1024:1152, :], mk)
    for u in range(QB // 128):
        r = slice(u * 128, (u + 1) * 128)
        tot = jnp.sum(l[r, :], axis=1, keepdims=True)
        o_ref[r, :] = (acc[r, :] / tot).astype(jnp.bfloat16)
        lse = m[r, :] * CS + jnp.log2(tot)
        lse_ref[0, u, :] = jnp.transpose(lse)[0, :]

def attention(scal, q, ks, vs, QB=2048, SB=1024, KB=512):
    rows = q.shape[0]; nsh = len(ks)
    full = lambda a: pl.BlockSpec(a.shape, lambda i: (0, 0))
    o, lse = pl.pallas_call(
        functools.partial(attn_kernel, nsh, QB, SB, KB),
        grid=(rows // QB,),
        in_specs=[pl.BlockSpec(memory_space=pltpu.SMEM), pl.BlockSpec((QB, 128), lambda i: (i, 0))] + [full(a) for a in ks + vs],
        out_specs=[pl.BlockSpec((QB, 128), lambda i: (i, 0)), pl.BlockSpec((1, QB // 128, 128), lambda i: (i, 0, 0))],
        out_shape=[jax.ShapeDtypeStruct((rows, 128), jnp.bfloat16), jax.ShapeDtypeStruct((rows // QB, QB // 128, 128), jnp.float32)],
        scratch_shapes=[pltpu.SMEM((nsh,), jnp.int32)] + [pltpu.VMEM((QB, 128), jnp.float32)] * 3,
        compiler_params=pltpu.CompilerParams(dimension_semantics=("arbitrary",), vmem_limit_bytes=40 * 2**20),
    )(scal, q, *ks, *vs)
    return o, lse


def merge_kernel(p1, p2, l1, l2, o, lo):
    for u in range(p1.shape[0] // 128):
        r = slice(u * 128, (u + 1) * 128)
        a, b = l1[u : u + 1, :], l2[u : u + 1, :]
        top = jnp.maximum(a, b)
        ea, eb = jnp.exp2(a - top), jnp.exp2(b - top)
        tot = ea + eb
        lo[u : u + 1, :] = top + jnp.log2(tot)
        wa = jnp.transpose(jnp.broadcast_to(ea / tot, (128, 128)))
        wb = jnp.transpose(jnp.broadcast_to(eb / tot, (128, 128)))
        o[r, :] = (p1[r, :].astype(jnp.float32) * wa + p2[r, :].astype(jnp.float32) * wb).astype(jnp.bfloat16)


def merge(p1, p2, l1, l2):
    return pl.pallas_call(
        merge_kernel,
        out_shape=[jax.ShapeDtypeStruct(p1.shape, jnp.bfloat16), jax.ShapeDtypeStruct(l1.shape, jnp.float32)],
    )(p1, p2, l1, l2)


def shift(v, axis, d):
    n = {"zh": 2, "x": 4, "c": 2, "y": 4, "zl": 2}[axis]
    return lax.ppermute(v, axis, [(i, (i + d) % n) for i in range(n)])


def f32(v):
    return v.astype(jnp.float32)


def bf16(v):
    return v.astype(jnp.bfloat16)


def x_ring(b):
    h = b.shape[0] // 2
    r, l = shift(b, "x", 1), shift(b, "x", -1)
    return [(-1, 0, r), (1, 0, l), (2, 0, shift(r[:h], "x", 1)), (2, h, shift(l[h:], "x", -1))]


def scatter_sums(v):
    own, p1, p2, m1 = v[0], v[1], v[2], v[3]
    h = v.shape[2] // 2
    a = shift(p2[:, :h], "y", 1)
    b = shift(p2[:, h:], "y", -1)
    c = shift(p1[:, h:], "y", 1)
    d = shift(m1[:, :h], "y", -1)
    e = shift(bf16(f32(p1[:, :h]) + f32(a)), "y", 1)
    g = shift(bf16(f32(m1[:, h:]) + f32(b)), "y", -1)
    low = f32(own[:, :h]) + f32(e) + f32(d)
    high = f32(own[:, h:]) + f32(c) + f32(g)
    away = jnp.concatenate([bf16(low[1]), bf16(high[1])], 0)
    z = f32(shift(away, "zl", 1))
    return bf16(jnp.concatenate([low[0] + z[:h], high[0] + z[h:]], 0))


def on_device(queries, fresh_keys, fresh_values, cache_keys, cache_values, lengths, segment, weight):
    zh, x, c, y, zl = [lax.axis_index(a) for a in ("zh", "x", "c", "y", "zl")]
    n = lengths[0]
    rows = lambda a: a.reshape(-1, 128)
    marks = jnp.concatenate([jnp.full((8, 128), n // 16, jnp.bfloat16), jnp.full((8, 128), n % 16, jnp.bfloat16)], 0)
    k0 = jnp.concatenate([rows(cache_keys), rows(fresh_keys), marks], 0)
    v0 = jnp.concatenate([rows(cache_values), rows(fresh_values)], 0)
    kr, kl, vr, vl = shift(k0, "x", 1), shift(k0, "x", -1), shift(v0, "x", 1), shift(v0, "x", -1)
    ko, vo = shift(kr, "x", 1), shift(vl, "x", -1)
    q0 = rows(queries)
    qc, qz = shift(q0, "c", 1), shift(q0, "zh", 1)
    qzc = shift(qz, "c", 1)
    q = jnp.concatenate([q0, qz, qc, qzc], 0)
    starts = [jnp.int32(0)] + [jnp.sum((segment < g).astype(jnp.int32)) for g in (1, 2, 3)]
    first = lambda zz, xx, cc: ((zz * 4 + xx % 4) * 2 + cc) * 128
    scal = jnp.stack(
        starts
        + [first(zh, x + d, c) for d in (0, 3, 1, 2)]
        + [first(zh, x, c), first(1 - zh, x, c), first(zh, x, 1 - c), first(1 - zh, x, 1 - c)]
    ).astype(jnp.int32)
    part, lse = attention(scal, q, [k0, kr, kl, ko], [v0, vr, vl, vo])
    lse = lse.reshape(64, 128)
    m1, l1 = merge(part[:4096], shift(part[4096:], "c", 1), lse[:32], shift(lse[32:], "c", 1))
    att, _ = merge(m1[:2048], shift(m1[2048:], "zh", 1), l1[:16], shift(l1[16:], "zh", 1))
    attended = att.reshape(128, 16, 128)

    a = attended.reshape(128, 2048)
    az = shift(a, "zh", 1)
    blocks = [(zh, 0, 0, a)] + [(zh,) + t for t in x_ring(a)]
    blocks += [(1 - zh, 0, 0, az)] + [(1 - zh,) + t for t in x_ring(az)]
    arr = jnp.zeros((8, 128, 2048), jnp.bfloat16)
    for zz, dx, row, blk in blocks:
        xx = (x + dx) % 4
        slot = ((zz * 2 + xx // 2 - y) % 4) * 2 + (xx % 2 + zl) % 2
        arr = lax.dynamic_update_slice(arr, blk[None], (slot, row, 0))
    arr = arr.reshape(1024, 2048)
    far = shift(weight, "c", 1)
    dot = lambda w: bf16(jnp.dot(arr, w, preferred_element_type=jnp.float32)).reshape(4, 2, 128, 1024)
    theirs = shift(scatter_sums(dot(far)), "c", 1)
    mine = scatter_sums(dot(weight))
    mixed = jnp.where(c == 0, jnp.concatenate([mine, theirs], 0), jnp.concatenate([theirs, mine], 0))
    return attended, mixed


def solution(mesh):
    fine = Mesh(mesh.devices.reshape(2, 4, 2, 4, 2), ("zh", "x", "c", "y", "zl"))
    ctx, tp = ("zh", "x", "c"), ("y", "zl")
    heads = P(ctx, tp, None)
    return jax.shard_map(
        on_device,
        mesh=fine,
        in_specs=(heads, heads, heads, heads, heads, P(ctx), P(), P(tp, ctx)),
        out_specs=(heads, P(tp, ctx)),
        check_vma=False,
    )
```

```python
import functools
import math

import jax
import jax.numpy as jnp
from jax import lax
from jax.experimental import pallas as pl
from jax.experimental.pallas import tpu as pltpu
from jax.sharding import Mesh, PartitionSpec as P

NEG = -1e30
CS = math.log2(math.e) / math.sqrt(128.0)
NT = (((1,), (1,)), ((), ()))
R = 1024
RP = R + 48
SB = 512
KB = 512
TN = 512


def f32(v):
    return v.astype(jnp.float32)


def bf16(v):
    return v.astype(jnp.bfloat16)


def first(zh, x, c):
    return ((zh * 4 + x % 4) * 2 + c) * 128


def load_log(ref, b):
    return f32(ref[b, R : R + 8, :]) + f32(ref[b, R + 16 : R + 24, :]) + f32(ref[b, R + 32 : R + 40, :])


def store_log(ref, b, v):
    v = jnp.concatenate([v, jnp.zeros_like(v)], 0)
    for i in range(3):
        piece = bf16(v)
        ref[b, R + 16 * i : R + 16 * (i + 1), :] = piece
        v = v - f32(piece)


def spread(row):
    return jnp.transpose(jnp.broadcast_to(row, (128, 128)))


def attn_kernel(nsh, kvs, dxs, group, chained, seg, q_ref, *rest):
    n_in = sum(len(t) for t in kvs)
    kv_refs, rest = rest[:n_in], list(rest[n_in:])
    init = rest.pop(0) if chained else None
    o_ref, lens, firsts, kst, vst, m, l, acc = rest
    zh, x, c = lax.axis_index("zh"), lax.axis_index("x"), lax.axis_index("c")
    at = 0
    for s, t in enumerate(kvs):
        k = kv_refs[at]
        kst[s] = k[0:1152, :]
        mark = f32(k[1152:1168, :])
        lens[s] = (jnp.max(mark[0:8]) * 16.0 + jnp.max(mark[8:16])).astype(jnp.int32)
        firsts[s] = first(zh, x + dxs[s], c)
        vst[s] = k[1168:2320, :] if len(t) == 1 else kv_refs[at + 1][...]
        at += len(t)
    starts = [jnp.int32(0)] + [jnp.sum((seg[...] < g).astype(jnp.int32)) for g in (1, 2, 3)]

    if chained:
        for b in range(2):
            logs = load_log(init, b) * (1.0 / CS)
            for u in range(R // 128):
                r = slice(b * R + u * 128, b * R + (u + 1) * 128)
                m[r, :] = spread(logs[u : u + 1, :])
                acc[r, :] = f32(init[b, u * 128 : (u + 1) * 128, :])
        l[...] = jnp.full(l.shape, 1.0 / 128.0, jnp.float32)
    else:
        m[...] = jnp.full(m.shape, NEG, jnp.float32)
        l[...] = jnp.zeros(l.shape, jnp.float32)
        acc[...] = jnp.zeros(acc.shape, jnp.float32)
    base = first((zh + group[0]) % 2, x, (c + group[1]) % 2)
    bases = [base, base + 64]

    def seen_from(pos, like):
        lo = jnp.zeros_like(like)
        for g in range(1, 4):
            lo = jnp.where(starts[g] <= pos, starts[g], lo)
        return lo

    U = 2 * R // SB
    H = R // SB

    def step(k, v, masks):
        n = k.shape[0] // 128

        def qk(u):
            q = q_ref[u // H, (u % H) * SB : (u % H + 1) * SB, :]
            s = lax.dot_general(q, k, NT, preferred_element_type=jnp.float32)
            return s if masks is None else jnp.where(masks(u), s, NEG)

        def soft(u, s):
            r = slice(u * SB, (u + 1) * SB)
            mp = m[r, :]
            mn = jnp.maximum(mp, jnp.max(s, axis=1, keepdims=True))
            al = jnp.exp2((mp - mn) * CS)
            ps = [jnp.exp2((s[:, j * 128 : (j + 1) * 128] - mn) * CS) for j in range(n)]
            tot = ps[0]
            for p in ps[1:]:
                tot = tot + p
            l[r, :] = l[r, :] * al + tot
            m[r, :] = mn
            return al, jnp.concatenate([bf16(p) for p in ps], axis=1) if n > 1 else bf16(ps[0])

        def pv(u, al, p):
            r = slice(u * SB, (u + 1) * SB)
            acc[r, :] = acc[r, :] * al + jnp.dot(p, v, preferred_element_type=jnp.float32)

        s = qk(0)
        prev = None
        for u in range(U):
            nxt = qk(u + 1) if u + 1 < U else None
            cur = soft(u, s)
            if prev is not None:
                pv(u - 1, *prev)
            prev, s = cur, nxt
        pv(U - 1, *prev)

    @pl.loop(0, nsh)
    def _(s):
        k_ref, v_ref, n = kst.at[s], vst.at[s], lens[s]
        full = n // KB

        @pl.loop(0, full)
        def _(j):
            o = pl.multiple_of(j * KB, KB)
            step(k_ref[pl.ds(o, KB), :], v_ref[pl.ds(o, KB), :], None)

        rem = n - full * KB
        below = 0
        for size in (KB // 2, KB):

            @pl.when((rem > below) & (rem <= size))
            def _():
                o = pl.multiple_of(full * KB, KB)
                lane = lax.broadcasted_iota(jnp.int32, (SB, size), 1) + o
                step(k_ref[pl.ds(o, size), :], v_ref[pl.ds(o, size), :], lambda u: lane < n)

            below = size
        f = firsts[s]
        any_seen = False
        for b in bases:
            any_seen = any_seen | ((f <= b + (R // 16 - 1)) & (f + 127 >= seen_from(b, b)))

        @pl.when(any_seen)
        def _():
            def mk(u):
                qp = bases[u // H] + (u % H) * (SB // 16) + lax.broadcasted_iota(jnp.int32, (SB, 128), 0) // 16
                kp = f + lax.broadcasted_iota(jnp.int32, (SB, 128), 1)
                return (kp <= qp) & (kp >= seen_from(qp, qp))

            step(k_ref[1024:1152, :], v_ref[1024:1152, :], mk)

    for b in range(2):
        logs = []
        for u in range(R // 128):
            r = slice(b * R + u * 128, b * R + (u + 1) * 128)
            tot = jnp.sum(l[r, :], axis=1, keepdims=True)
            o_ref[b, u * 128 : (u + 1) * 128, :] = bf16(acc[r, :] / tot)
            logs.append(jnp.transpose(m[r, :] * CS + jnp.log2(tot))[0:1, :])
        store_log(o_ref, b, jnp.concatenate(logs, 0))


def attention(seg, q, group, kvs, dxs, init):
    nsh = len(kvs)
    flat = [a for t in kvs for a in t]
    elements = 2 * R * nsh * 640
    return pl.pallas_call(
        functools.partial(attn_kernel, nsh, kvs, dxs, group, init is not None),
        out_shape=jax.ShapeDtypeStruct((2, RP, 128), jnp.bfloat16),
        scratch_shapes=[pltpu.SMEM((nsh,), jnp.int32)] * 2
        + [pltpu.VMEM((nsh, 1152, 128), jnp.bfloat16)] * 2
        + [pltpu.VMEM((2 * R, 128), jnp.float32)] * 3,
        compiler_params=pltpu.CompilerParams(vmem_limit_bytes=32 * 2**20),
        cost_estimate=pl.CostEstimate(flops=elements * 2400, bytes_accessed=2 * R * 512, transcendentals=elements),
    )(seg, q, *flat, *([init] if init is not None else []))


def weigh(refs, bs):
    logs = [load_log(r, b) for r, b in zip(refs, bs)]
    top = functools.reduce(jnp.maximum, logs)
    es = [jnp.exp2(v - top) for v in logs]
    tot = functools.reduce(jnp.add, es)
    return [e / tot for e in es], top + jnp.log2(tot)


def mix(refs, bs, ws, u):
    r = slice(u * 128, (u + 1) * 128)
    return functools.reduce(jnp.add, [f32(x[b, r, :]) * spread(w[u : u + 1, :]) for x, b, w in zip(refs, bs, ws)])


def merge_kernel(a, b, o):
    for j in range(o.shape[0]):
        ws, logs = weigh((a, b), (j, j))
        store_log(o, j, logs)
        for u in range(R // 128):
            o[j, u * 128 : (u + 1) * 128, :] = bf16(mix((a, b), (j, j), ws, u))


def merge(a, b):
    return pl.pallas_call(merge_kernel, out_shape=jax.ShapeDtypeStruct((2, RP, 128), jnp.bfloat16))(a, b)


def last_merge_kernel(a, b, z, att, flat0, flat1, hold):
    for j, flat in enumerate((flat0, flat1)):
        refs, bs = (a, b, z), (j, j, j)
        ws, _ = weigh(refs, bs)
        for u in range(R // 128):
            v = mix(refs, bs, ws, u)
            hold[u * 128 : (u + 1) * 128, :] = v
            att[j * R + u * 128 : j * R + (u + 1) * 128, :] = bf16(v)
        for h in range(16):
            flat[:, h * 128 : (h + 1) * 128] = bf16(hold[pl.ds(h, R // 16, stride=16), :])


def last_merge(a, b, z):
    return pl.pallas_call(
        last_merge_kernel,
        out_shape=[jax.ShapeDtypeStruct((2 * R, 128), jnp.bfloat16)]
        + [jax.ShapeDtypeStruct((R // 16, 2048), jnp.bfloat16)] * 2,
        scratch_shapes=[pltpu.VMEM((R, 128), jnp.float32)],
    )(a, b, z)


def project_kernel(slots, *refs):
    blocks, (near, far), outs, arr = refs[:8], refs[8:10], refs[10:18], refs[18]
    j = pl.program_id(0)

    @pl.when(j == 0)
    def _():
        for i in range(8):
            arr[slots[i]] = blocks[i][...]

    def go(w):
        t = blocks[0].shape[0]
        p = jnp.dot(arr[...].reshape(8 * t, 2048), w[...], preferred_element_type=jnp.float32)
        for i in range(8):
            outs[i][...] = bf16(p[i * t : (i + 1) * t])

    pl.when(j < 1024 // TN)(lambda: go(near))
    pl.when(j >= 1024 // TN)(lambda: go(far))


def project(slots, blocks, near, far):
    t = blocks[0].shape[0]
    block = pl.BlockSpec((t, 2048), lambda j: (0, 0))
    return pl.pallas_call(
        project_kernel,
        grid=(2048 // TN,),
        in_specs=[pl.BlockSpec(memory_space=pltpu.SMEM)]
        + [block] * 8
        + [
            pl.BlockSpec((2048, TN), lambda j: (0, jnp.minimum(j, 1024 // TN - 1))),
            pl.BlockSpec((2048, TN), lambda j: (0, jnp.maximum(j - 1024 // TN, 0))),
        ],
        out_specs=[pl.BlockSpec((t, TN), lambda j: (0, j))] * 8,
        out_shape=[jax.ShapeDtypeStruct((t, 2048), jnp.bfloat16)] * 8,
        scratch_shapes=[pltpu.VMEM((8, t, 2048), jnp.bfloat16)],
        compiler_params=pltpu.CompilerParams(dimension_semantics=("arbitrary",), vmem_limit_bytes=32 * 2**20),
        cost_estimate=pl.CostEstimate(flops=2 * 8 * t * 2048 * 2048, bytes_accessed=8 * 2**20, transcendentals=0),
    )(slots, *blocks, near, far)


def shift(v, axis, d):
    n = {"zh": 2, "x": 4, "c": 2, "y": 4, "zl": 2}[axis]
    return lax.ppermute(v, axis, [(i, (i + d) % n) for i in range(n)])


def scatter_sums(v):
    own, p1, p2, m1 = v[0:2], v[2:4], v[4:6], v[6:8]
    a, b = shift(p2[0], "y", 1), shift(p2[1], "y", -1)
    c, d = shift(p1[1], "y", 1), shift(m1[0], "y", -1)
    e = shift(bf16(f32(p1[0]) + f32(a)), "y", 1)
    g = shift(bf16(f32(m1[1]) + f32(b)), "y", -1)
    keep = f32(own[0]) + f32(e) + f32(d)
    away = shift(bf16(f32(own[1]) + f32(c) + f32(g)), "zl", 1)
    return keep + f32(away)


def on_device(queries, fresh_keys, fresh_values, cache_keys, cache_values, lengths, segment, weight):
    zh, x, c, y, zl = [lax.axis_index(a) for a in ("zh", "x", "c", "y", "zl")]
    n = lengths[0]
    rows = lambda a: a.reshape(-1, 128)
    marks = jnp.concatenate([jnp.full((8, 128), n // 16, jnp.bfloat16), jnp.full((8, 128), n % 16, jnp.bfloat16)], 0)
    kv = jnp.concatenate([rows(cache_keys), rows(fresh_keys), marks, rows(cache_values), rows(fresh_values)], 0)
    q0 = queries.reshape(2, R, 128)
    qc = shift(q0, "c", 1)
    right, left = shift(kv, "x", 1), shift(kv, "x", -1)
    qz = shift(q0, "zh", 1)
    qzc = shift(qz, "c", 1)
    ko, vo = shift(right[:1168], "x", 1), shift(left[1168:], "x", -1)
    far = shift(weight, "c", 1)

    seg = segment.reshape(16, 128)
    rest, dxs = [(right,), (left,), (ko, vo)], (3, 1, 2)
    near = lambda q, group: attention(seg, q, group, [(kv,)], (0,), None)
    p0, pc = near(q0, (0, 0)), near(qc, (0, 1))
    pz, pzc = near(qz, (1, 0)), near(qzc, (1, 1))
    done = lambda q, group, init: attention(seg, q, group, rest, dxs, init)
    dzc = done(qzc, (1, 1), pzc)
    zc_in = shift(dzc, "c", 1)
    pz, _ = lax.optimization_barrier((pz, dzc))
    dz = done(qz, (1, 0), pz)
    chip_far = merge(dz, zc_in)
    from_z = shift(chip_far, "zh", 1)
    pc, _ = lax.optimization_barrier((pc, chip_far))
    dc = done(qc, (0, 1), pc)
    c_in = shift(dc, "c", 1)
    p0, _ = lax.optimization_barrier((p0, dc))
    d0 = done(q0, (0, 0), p0)
    att, *flats = last_merge(d0, c_in, from_z)

    slots = []
    for zz, dx in [(zh, 0), (zh, 3), (zh, 1), (zh, 2), (1 - zh, 0), (1 - zh, 3), (1 - zh, 1), (1 - zh, 2)]:
        xx = (x + dx) % 4
        slots.append(((zz * 2 + xx // 2 - y) % 4) * 2 + (xx % 2 + zl) % 2)
    slots = jnp.stack(slots).astype(jnp.int32)

    sums = []
    for j, a in enumerate(flats):
        az = shift(a, "zh", 1)
        r, le = shift(a, "x", 1), shift(a, "x", -1)
        rz, lz = shift(az, "x", 1), shift(az, "x", -1)
        o = shift(le if j else r, "x", -1 if j else 1)
        oz = shift(o, "zh", 1)
        sums.append(scatter_sums(project(slots, [a, r, le, o, az, rz, lz, oz], weight, far)))
    attended = att.reshape(128, 16, 128)
    whole = bf16(jnp.concatenate(sums, 0))
    mine, theirs = whole[:, :1024], shift(whole[:, 1024:], "c", 1)
    mixed = jnp.where(c == 0, jnp.concatenate([mine, theirs], 0), jnp.concatenate([theirs, mine], 0))
    return attended, mixed


def solution(mesh):
    fine = Mesh(mesh.devices.reshape(2, 4, 2, 4, 2), ("zh", "x", "c", "y", "zl"))
    ctx, tp = ("zh", "x", "c"), ("y", "zl")
    heads = P(ctx, tp, None)
    return jax.shard_map(
        on_device,
        mesh=fine,
        in_specs=(heads, heads, heads, heads, heads, P(ctx), P(), P(tp, ctx)),
        out_specs=(heads, P(tp, ctx)),
        check_vma=False,
    )
```

```python
import functools
import math

import jax
import jax.numpy as jnp
from jax import lax
from jax.experimental import pallas as pl
from jax.experimental.pallas import tpu as pltpu
from jax.sharding import Mesh, PartitionSpec as P

NEG = -1e30
CS = math.log2(math.e) / math.sqrt(128.0)
NT = (((1,), (1,)), ((), ()))
R = 1024
RP = R + 48
SB = 512
KB = 512


def f32(v):
    return v.astype(jnp.float32)


def bf16(v):
    return v.astype(jnp.bfloat16)


def first(zh, x, c):
    return ((zh * 4 + x % 4) * 2 + c) * 128


def load_log(ref, b):
    return f32(ref[b, R : R + 8, :]) + f32(ref[b, R + 16 : R + 24, :]) + f32(ref[b, R + 32 : R + 40, :])


def store_log(ref, b, v):
    v = jnp.concatenate([v, jnp.zeros_like(v)], 0)
    for i in range(3):
        piece = bf16(v)
        ref[b, R + 16 * i : R + 16 * (i + 1), :] = piece
        v = v - f32(piece)


def spread(row):
    return jnp.transpose(jnp.broadcast_to(row, (128, 128)))


def attn_kernel(nsh, kvs, dxs, group, chained, seg, q_ref, *rest):
    n_in = sum(len(t) for t in kvs)
    kv_refs, rest = rest[:n_in], list(rest[n_in:])
    init = rest.pop(0) if chained else None
    o_ref, lens, firsts, kst, vst, m, l, acc = rest
    zh, x, c = lax.axis_index("zh"), lax.axis_index("x"), lax.axis_index("c")
    at = 0
    for s, t in enumerate(kvs):
        k = kv_refs[at]
        kst[s] = k[0:1152, :]
        mark = f32(k[1152:1168, :])
        lens[s] = (jnp.max(mark[0:8]) * 16.0 + jnp.max(mark[8:16])).astype(jnp.int32)
        firsts[s] = first(zh, x + dxs[s], c)
        vst[s] = k[1168:2320, :] if len(t) == 1 else kv_refs[at + 1][...]
        at += len(t)
    starts = [jnp.int32(0)] + [jnp.sum((seg[...] < g).astype(jnp.int32)) for g in (1, 2, 3)]

    if chained:
        for b in range(2):
            logs = load_log(init, b) * (1.0 / CS)
            for u in range(R // 128):
                r = slice(b * R + u * 128, b * R + (u + 1) * 128)
                m[r, :] = spread(logs[u : u + 1, :])
                acc[r, :] = f32(init[b, u * 128 : (u + 1) * 128, :])
        l[...] = jnp.full(l.shape, 1.0 / 128.0, jnp.float32)
    else:
        m[...] = jnp.full(m.shape, NEG, jnp.float32)
        l[...] = jnp.zeros(l.shape, jnp.float32)
        acc[...] = jnp.zeros(acc.shape, jnp.float32)
    base = first((zh + group[0]) % 2, x, (c + group[1]) % 2)
    bases = [base, base + 64]

    def seen_from(pos, like):
        lo = jnp.zeros_like(like)
        for g in range(1, 4):
            lo = jnp.where(starts[g] <= pos, starts[g], lo)
        return lo

    U = 2 * R // SB
    H = R // SB

    def step(k, v, masks):
        n = k.shape[0] // 128

        def qk(u):
            q = q_ref[u // H, (u % H) * SB : (u % H + 1) * SB, :]
            s = lax.dot_general(q, k, NT, preferred_element_type=jnp.float32)
            return s if masks is None else jnp.where(masks(u), s, NEG)

        def soft(u, s):
            r = slice(u * SB, (u + 1) * SB)
            mp = m[r, :]
            mn = jnp.maximum(mp, jnp.max(s, axis=1, keepdims=True))
            al = jnp.exp2((mp - mn) * CS)
            ps = [jnp.exp2((s[:, j * 128 : (j + 1) * 128] - mn) * CS) for j in range(n)]
            tot = ps[0]
            for p in ps[1:]:
                tot = tot + p
            l[r, :] = l[r, :] * al + tot
            m[r, :] = mn
            return al, jnp.concatenate([bf16(p) for p in ps], axis=1) if n > 1 else bf16(ps[0])

        def pv(u, al, p):
            r = slice(u * SB, (u + 1) * SB)
            acc[r, :] = acc[r, :] * al + jnp.dot(p, v, preferred_element_type=jnp.float32)

        s = qk(0)
        prev = None
        for u in range(U):
            nxt = qk(u + 1) if u + 1 < U else None
            cur = soft(u, s)
            if prev is not None:
                pv(u - 1, *prev)
            prev, s = cur, nxt
        pv(U - 1, *prev)

    @pl.loop(0, nsh)
    def _(s):
        k_ref, v_ref, n = kst.at[s], vst.at[s], lens[s]
        full = n // KB

        @pl.loop(0, full)
        def _(j):
            o = pl.multiple_of(j * KB, KB)
            step(k_ref[pl.ds(o, KB), :], v_ref[pl.ds(o, KB), :], None)

        rem = n - full * KB
        below = 0
        for size in (128, 256, 384, 512):

            @pl.when((rem > below) & (rem <= size))
            def _():
                o = pl.multiple_of(full * KB, KB)
                lane = lax.broadcasted_iota(jnp.int32, (SB, size), 1) + o
                step(k_ref[pl.ds(o, size), :], v_ref[pl.ds(o, size), :], lambda u: lane < n)

            below = size
        f = firsts[s]
        any_seen = False
        for b in bases:
            any_seen = any_seen | ((f <= b + (R // 16 - 1)) & (f + 127 >= seen_from(b, b)))

        @pl.when(any_seen)
        def _():
            def mk(u):
                qp = bases[u // H] + (u % H) * (SB // 16) + lax.broadcasted_iota(jnp.int32, (SB, 128), 0) // 16
                kp = f + lax.broadcasted_iota(jnp.int32, (SB, 128), 1)
                return (kp <= qp) & (kp >= seen_from(qp, qp))

            step(k_ref[1024:1152, :], v_ref[1024:1152, :], mk)

    for b in range(2):
        logs = []
        for u in range(R // 128):
            r = slice(b * R + u * 128, b * R + (u + 1) * 128)
            tot = jnp.sum(l[r, :], axis=1, keepdims=True)
            o_ref[b, u * 128 : (u + 1) * 128, :] = bf16(acc[r, :] / tot)
            logs.append(jnp.transpose(m[r, :] * CS + jnp.log2(tot))[0:1, :])
        store_log(o_ref, b, jnp.concatenate(logs, 0))


def attention(seg, q, group, kvs, dxs, init):
    nsh = len(kvs)
    flat = [a for t in kvs for a in t]
    elements = 2 * R * nsh * 640
    return pl.pallas_call(
        functools.partial(attn_kernel, nsh, kvs, dxs, group, init is not None),
        out_shape=jax.ShapeDtypeStruct((2, RP, 128), jnp.bfloat16),
        scratch_shapes=[pltpu.SMEM((nsh,), jnp.int32)] * 2
        + [pltpu.VMEM((nsh, 1152, 128), jnp.bfloat16)] * 2
        + [pltpu.VMEM((2 * R, 128), jnp.float32)] * 3,
        compiler_params=pltpu.CompilerParams(vmem_limit_bytes=32 * 2**20),
        cost_estimate=pl.CostEstimate(flops=elements * 2400, bytes_accessed=2 * R * 512, transcendentals=elements),
    )(seg, q, *flat, *([init] if init is not None else []))


def weigh(refs, bs):
    logs = [load_log(r, b) for r, b in zip(refs, bs)]
    top = functools.reduce(jnp.maximum, logs)
    es = [jnp.exp2(v - top) for v in logs]
    tot = functools.reduce(jnp.add, es)
    return [e / tot for e in es], top + jnp.log2(tot)


def mix(refs, bs, ws, u):
    r = slice(u * 128, (u + 1) * 128)
    return functools.reduce(jnp.add, [f32(x[b, r, :]) * spread(w[u : u + 1, :]) for x, b, w in zip(refs, bs, ws)])


def merge_kernel(a, b, o):
    for j in range(o.shape[0]):
        ws, logs = weigh((a, b), (j, j))
        store_log(o, j, logs)
        for u in range(R // 128):
            o[j, u * 128 : (u + 1) * 128, :] = bf16(mix((a, b), (j, j), ws, u))


def merge(a, b):
    return pl.pallas_call(merge_kernel, out_shape=jax.ShapeDtypeStruct((2, RP, 128), jnp.bfloat16))(a, b)


def last_merge_kernel(a, b, z, att, flat0, flat1, hold):
    for j, flat in enumerate((flat0, flat1)):
        refs, bs = (a, b, z), (j, j, j)
        ws, _ = weigh(refs, bs)
        for u in range(R // 128):
            v = mix(refs, bs, ws, u)
            hold[u * 128 : (u + 1) * 128, :] = v
            att[j * R + u * 128 : j * R + (u + 1) * 128, :] = bf16(v)
        for h in range(16):
            flat[:, h * 128 : (h + 1) * 128] = bf16(hold[pl.ds(h, R // 16, stride=16), :])


def last_merge(a, b, z):
    return pl.pallas_call(
        last_merge_kernel,
        out_shape=[jax.ShapeDtypeStruct((2 * R, 128), jnp.bfloat16)]
        + [jax.ShapeDtypeStruct((R // 16, 2048), jnp.bfloat16)] * 2,
        scratch_shapes=[pltpu.VMEM((R, 128), jnp.float32)],
    )(a, b, z)


def assemble_kernel(slots, *refs):
    out, low = refs[-1], 0
    if len(refs) > 9:
        low = refs[8].shape[1]
        out[:, 0:low, :] = refs[8][...]
    for i, block in enumerate(refs[:8]):
        out[slots[i], low : low + block.shape[0], :] = block[...]


def assemble(slots, blocks, before):
    parts = blocks + ([] if before is None else [before])
    rows = blocks[0].shape[0] + (0 if before is None else before.shape[1])
    return pl.pallas_call(
        assemble_kernel,
        in_specs=[pl.BlockSpec(memory_space=pltpu.SMEM)] + [pl.BlockSpec(memory_space=pltpu.VMEM)] * len(parts),
        out_shape=jax.ShapeDtypeStruct((8, rows, 2048), jnp.bfloat16),
        compiler_params=pltpu.CompilerParams(vmem_limit_bytes=16 * 2**20),
    )(slots, *parts)


def pack_kernel(n, ck, fk, cv, fv, kv):
    kv[0:1024, :] = ck[...]
    kv[1024:1152, :] = fk[...]
    row = lax.broadcasted_iota(jnp.int32, (16, 128), 0)
    kv[1152:1168, :] = bf16(f32(jnp.where(row < 8, n[0] // 16, n[0] % 16)))
    kv[1168:2192, :] = cv[...]
    kv[2192:2320, :] = fv[...]


def pack(n, *parts):
    return pl.pallas_call(
        pack_kernel,
        in_specs=[pl.BlockSpec(memory_space=pltpu.SMEM)] + [pl.BlockSpec(memory_space=pltpu.VMEM)] * 4,
        out_shape=jax.ShapeDtypeStruct((2320, 128), jnp.bfloat16),
    )(n, *parts)


def shift(v, axis, d):
    n = {"zh": 2, "x": 4, "c": 2, "y": 4, "zl": 2}[axis]
    return lax.ppermute(v, axis, [(i, (i + d) % n) for i in range(n)])


def scatter_sums(v):
    own, p1, p2, m1 = v[0:2], v[2:4], v[4:6], v[6:8]
    a, b = shift(p2[0], "y", 1), shift(p2[1], "y", -1)
    c, d = shift(p1[1], "y", 1), shift(m1[0], "y", -1)
    e = shift(bf16(f32(p1[0]) + f32(a)), "y", 1)
    g = shift(bf16(f32(m1[1]) + f32(b)), "y", -1)
    keep = f32(own[0]) + f32(e) + f32(d)
    away = shift(bf16(f32(own[1]) + f32(c) + f32(g)), "zl", 1)
    return keep + f32(away)


def on_device(queries, fresh_keys, fresh_values, cache_keys, cache_values, lengths, segment, weight):
    zh, x, c, y, zl = [lax.axis_index(a) for a in ("zh", "x", "c", "y", "zl")]
    rows = lambda v: v.reshape(-1, 128)
    kv = pack(lengths, rows(cache_keys), rows(fresh_keys), rows(cache_values), rows(fresh_values))
    q0 = queries.reshape(2, R, 128)
    right, left = shift(kv, "x", 1), shift(kv, "x", -1)
    qc = shift(q0, "c", 1)
    qz = shift(q0, "zh", 1)
    qzc = shift(qz, "c", 1)
    ko, vo = shift(right[:1168], "x", 1), shift(left[1168:], "x", -1)
    far = shift(weight, "c", 1)

    seg = segment.reshape(16, 128)
    rest, dxs = [(right,), (left,), (ko, vo)], (3, 1, 2)
    near = lambda q, group: attention(seg, q, group, [(kv,)], (0,), None)
    p0, pc = near(q0, (0, 0)), near(qc, (0, 1))
    pz, pzc = near(qz, (1, 0)), near(qzc, (1, 1))
    done = lambda q, group, init: attention(seg, q, group, rest, dxs, init)
    dzc = done(qzc, (1, 1), pzc)
    zc_in = shift(dzc, "c", 1)
    pz, _ = lax.optimization_barrier((pz, dzc))
    dz = done(qz, (1, 0), pz)
    chip_far = merge(dz, zc_in)
    from_z = shift(chip_far, "zh", 1)
    pc, _ = lax.optimization_barrier((pc, chip_far))
    dc = done(qc, (0, 1), pc)
    c_in = shift(dc, "c", 1)
    p0, _ = lax.optimization_barrier((p0, dc))
    d0 = done(q0, (0, 0), p0)
    att, *flats = last_merge(d0, c_in, from_z)

    slots = []
    for zz, dx in [(zh, 0), (zh, 3), (zh, 1), (zh, 2), (1 - zh, 0), (1 - zh, 3), (1 - zh, 1), (1 - zh, 2)]:
        xx = (x + dx) % 4
        slots.append(((zz * 2 + xx // 2 - y) % 4) * 2 + (xx % 2 + zl) % 2)

    arr, slots = None, jnp.stack(slots).astype(jnp.int32)
    for j, a in enumerate(flats):
        az = shift(a, "zh", 1)
        r, le = shift(a, "x", 1), shift(a, "x", -1)
        rz, lz = shift(az, "x", 1), shift(az, "x", -1)
        o = shift(le if j else r, "x", -1 if j else 1)
        oz = shift(o, "zh", 1)
        arr = assemble(slots, [a, r, le, o, az, rz, lz, oz], arr)
    arr = arr.reshape(1024, 2048)
    dot = lambda w: bf16(jnp.dot(arr, w, preferred_element_type=jnp.float32)).reshape(8, 128, 1024)
    theirs = shift(bf16(scatter_sums(dot(far))), "c", 1)
    mine = bf16(scatter_sums(dot(weight)))
    attended = att.reshape(128, 16, 128)
    mixed = jnp.where(c == 0, jnp.concatenate([mine, theirs], 0), jnp.concatenate([theirs, mine], 0))
    return attended, mixed


def solution(mesh):
    fine = Mesh(mesh.devices.reshape(2, 4, 2, 4, 2), ("zh", "x", "c", "y", "zl"))
    ctx, tp = ("zh", "x", "c"), ("y", "zl")
    heads = P(ctx, tp, None)
    return jax.shard_map(
        on_device,
        mesh=fine,
        in_specs=(heads, heads, heads, heads, heads, P(ctx), P(), P(tp, ctx)),
        out_specs=(heads, P(tp, ctx)),
        check_vma=False,
    )
```

```python
import functools
import math

import jax
import jax.numpy as jnp
from jax import lax
from jax.experimental import pallas as pl
from jax.experimental.pallas import tpu as pltpu
from jax.sharding import Mesh, PartitionSpec as P

NEG = -1e30
CS = math.log2(math.e) / math.sqrt(128.0)
NT = (((1,), (1,)), ((), ()))
R = 1024
RP = R + 48
SB = 512
KB = 512


def f32(v):
    return v.astype(jnp.float32)


def bf16(v):
    return v.astype(jnp.bfloat16)


def first(zh, x, c):
    return ((zh * 4 + x % 4) * 2 + c) * 128


def load_log(ref, b):
    return f32(ref[b, R : R + 8, :]) + f32(ref[b, R + 16 : R + 24, :]) + f32(ref[b, R + 32 : R + 40, :])


def store_log(ref, b, v):
    v = jnp.concatenate([v, jnp.zeros_like(v)], 0)
    for i in range(3):
        piece = bf16(v)
        ref[b, R + 16 * i : R + 16 * (i + 1), :] = piece
        v = v - f32(piece)


def spread(row):
    return jnp.transpose(jnp.broadcast_to(row, (128, 128)))


def attn_kernel(nsh, kvs, dxs, group, chained, seg, q_ref, *rest):
    n_in = sum(len(t) for t in kvs)
    kv_refs, rest = rest[:n_in], list(rest[n_in:])
    init = rest.pop(0) if chained else None
    o_ref, lens, firsts, kst, vst, m, l, acc = rest
    zh, x, c = lax.axis_index("zh"), lax.axis_index("x"), lax.axis_index("c")
    at = 0
    for s, t in enumerate(kvs):
        k = kv_refs[at]
        kst[s] = k[0:1152, :]
        mark = f32(k[1152:1168, :])
        lens[s] = (jnp.max(mark[0:8]) * 16.0 + jnp.max(mark[8:16])).astype(jnp.int32)
        firsts[s] = first(zh, x + dxs[s], c)
        vst[s] = k[1168:2320, :] if len(t) == 1 else kv_refs[at + 1][...]
        at += len(t)
    starts = [jnp.int32(0)] + [jnp.sum((seg[...] < g).astype(jnp.int32)) for g in (1, 2, 3)]

    if chained:
        for b in range(2):
            logs = load_log(init, b) * (1.0 / CS)
            for u in range(R // 128):
                r = slice(b * R + u * 128, b * R + (u + 1) * 128)
                m[r, :] = spread(logs[u : u + 1, :])
                acc[r, :] = f32(init[b, u * 128 : (u + 1) * 128, :])
        l[...] = jnp.full(l.shape, 1.0 / 128.0, jnp.float32)
    else:
        m[...] = jnp.full(m.shape, NEG, jnp.float32)
        l[...] = jnp.zeros(l.shape, jnp.float32)
        acc[...] = jnp.zeros(acc.shape, jnp.float32)
    base = first((zh + group[0]) % 2, x, (c + group[1]) % 2)
    bases = [base, base + 64]

    def seen_from(pos, like):
        lo = jnp.zeros_like(like)
        for g in range(1, 4):
            lo = jnp.where(starts[g] <= pos, starts[g], lo)
        return lo

    U = 2 * R // SB
    H = R // SB

    def step(k, v, masks):
        n = k.shape[0] // 128

        def qk(u):
            q = q_ref[u // H, (u % H) * SB : (u % H + 1) * SB, :]
            s = lax.dot_general(q, k, NT, preferred_element_type=jnp.float32)
            return s if masks is None else jnp.where(masks(u), s, NEG)

        def soft(u, s):
            r = slice(u * SB, (u + 1) * SB)
            mp = m[r, :]
            mn = jnp.maximum(mp, jnp.max(s, axis=1, keepdims=True))
            al = jnp.exp2((mp - mn) * CS)
            ps = [jnp.exp2((s[:, j * 128 : (j + 1) * 128] - mn) * CS) for j in range(n)]
            tot = ps[0]
            for p in ps[1:]:
                tot = tot + p
            l[r, :] = l[r, :] * al + tot
            m[r, :] = mn
            return al, jnp.concatenate([bf16(p) for p in ps], axis=1) if n > 1 else bf16(ps[0])

        def pv(u, al, p):
            r = slice(u * SB, (u + 1) * SB)
            acc[r, :] = acc[r, :] * al + jnp.dot(p, v, preferred_element_type=jnp.float32)

        s = qk(0)
        prev = None
        for u in range(U):
            nxt = qk(u + 1) if u + 1 < U else None
            cur = soft(u, s)
            if prev is not None:
                pv(u - 1, *prev)
            prev, s = cur, nxt
        pv(U - 1, *prev)

    @pl.loop(0, nsh)
    def _(s):
        k_ref, v_ref, n = kst.at[s], vst.at[s], lens[s]
        full = n // KB

        @pl.loop(0, full)
        def _(j):
            o = pl.multiple_of(j * KB, KB)
            step(k_ref[pl.ds(o, KB), :], v_ref[pl.ds(o, KB), :], None)

        rem = n - full * KB
        below = 0
        for size in (128, 256, 384, 512):

            @pl.when((rem > below) & (rem <= size))
            def _():
                o = pl.multiple_of(full * KB, KB)
                lane = lax.broadcasted_iota(jnp.int32, (SB, size), 1) + o
                step(k_ref[pl.ds(o, size), :], v_ref[pl.ds(o, size), :], lambda u: lane < n)

            below = size
        f = firsts[s]
        any_seen = False
        for b in bases:
            any_seen = any_seen | ((f <= b + (R // 16 - 1)) & (f + 127 >= seen_from(b, b)))

        @pl.when(any_seen)
        def _():
            def mk(u):
                qp = bases[u // H] + (u % H) * (SB // 16) + lax.broadcasted_iota(jnp.int32, (SB, 128), 0) // 16
                kp = f + lax.broadcasted_iota(jnp.int32, (SB, 128), 1)
                return (kp <= qp) & (kp >= seen_from(qp, qp))

            step(k_ref[1024:1152, :], v_ref[1024:1152, :], mk)

    for b in range(2):
        logs = []
        for u in range(R // 128):
            r = slice(b * R + u * 128, b * R + (u + 1) * 128)
            tot = jnp.sum(l[r, :], axis=1, keepdims=True)
            o_ref[b, u * 128 : (u + 1) * 128, :] = bf16(acc[r, :] / tot)
            logs.append(jnp.transpose(m[r, :] * CS + jnp.log2(tot))[0:1, :])
        store_log(o_ref, b, jnp.concatenate(logs, 0))


def attention(seg, q, group, kvs, dxs, init):
    nsh = len(kvs)
    flat = [a for t in kvs for a in t]
    elements = 2 * R * nsh * 640
    return pl.pallas_call(
        functools.partial(attn_kernel, nsh, kvs, dxs, group, init is not None),
        out_shape=jax.ShapeDtypeStruct((2, RP, 128), jnp.bfloat16),
        scratch_shapes=[pltpu.SMEM((nsh,), jnp.int32)] * 2
        + [pltpu.VMEM((nsh, 1152, 128), jnp.bfloat16)] * 2
        + [pltpu.VMEM((2 * R, 128), jnp.float32)] * 3,
        compiler_params=pltpu.CompilerParams(vmem_limit_bytes=32 * 2**20),
        cost_estimate=pl.CostEstimate(flops=elements * 2400, bytes_accessed=2 * R * 512, transcendentals=elements),
    )(seg, q, *flat, *([init] if init is not None else []))


def weigh(refs, bs):
    logs = [load_log(r, b) for r, b in zip(refs, bs)]
    top = functools.reduce(jnp.maximum, logs)
    es = [jnp.exp2(v - top) for v in logs]
    tot = functools.reduce(jnp.add, es)
    return [e / tot for e in es], top + jnp.log2(tot)


def mix(refs, bs, ws, u):
    r = slice(u * 128, (u + 1) * 128)
    return functools.reduce(jnp.add, [f32(x[b, r, :]) * spread(w[u : u + 1, :]) for x, b, w in zip(refs, bs, ws)])


def merge_kernel(a, b, o):
    for j in range(o.shape[0]):
        ws, logs = weigh((a, b), (j, j))
        store_log(o, j, logs)
        for u in range(R // 128):
            o[j, u * 128 : (u + 1) * 128, :] = bf16(mix((a, b), (j, j), ws, u))


def merge(a, b):
    return pl.pallas_call(merge_kernel, out_shape=jax.ShapeDtypeStruct((2, RP, 128), jnp.bfloat16))(a, b)


def last_merge_kernel(a, b, z, att, flat0, flat1, hold):
    for j, flat in enumerate((flat0, flat1)):
        refs, bs = (a, b, z), (j, j, j)
        ws, _ = weigh(refs, bs)
        for u in range(R // 128):
            v = mix(refs, bs, ws, u)
            hold[u * 128 : (u + 1) * 128, :] = v
            att[j * R + u * 128 : j * R + (u + 1) * 128, :] = bf16(v)
        for h in range(16):
            flat[:, h * 128 : (h + 1) * 128] = bf16(hold[pl.ds(h, R // 16, stride=16), :])


def last_merge(a, b, z):
    return pl.pallas_call(
        last_merge_kernel,
        out_shape=[jax.ShapeDtypeStruct((2 * R, 128), jnp.bfloat16)]
        + [jax.ShapeDtypeStruct((R // 16, 2048), jnp.bfloat16)] * 2,
        scratch_shapes=[pltpu.VMEM((R, 128), jnp.float32)],
    )(a, b, z)


def assemble_kernel(slots, *refs):
    out, low = refs[-1], 0
    if len(refs) > 9:
        low = refs[8].shape[1]
        out[:, 0:low, :] = refs[8][...]
    for i, block in enumerate(refs[:8]):
        out[slots[i], low : low + block.shape[0], :] = block[...]


def assemble(slots, blocks, before):
    parts = blocks + ([] if before is None else [before])
    rows = blocks[0].shape[0] + (0 if before is None else before.shape[1])
    return pl.pallas_call(
        assemble_kernel,
        in_specs=[pl.BlockSpec(memory_space=pltpu.SMEM)] + [pl.BlockSpec(memory_space=pltpu.VMEM)] * len(parts),
        out_shape=jax.ShapeDtypeStruct((8, rows, 2048), jnp.bfloat16),
        compiler_params=pltpu.CompilerParams(vmem_limit_bytes=16 * 2**20),
    )(slots, *parts)


def pack_kernel(n, ck, fk, cv, fv, kv):
    kv[0:1024, :] = ck[...]
    kv[1024:1152, :] = fk[...]
    row = lax.broadcasted_iota(jnp.int32, (16, 128), 0)
    kv[1152:1168, :] = bf16(f32(jnp.where(row < 8, n[0] // 16, n[0] % 16)))
    kv[1168:2192, :] = cv[...]
    kv[2192:2320, :] = fv[...]


def pack(n, *parts):
    return pl.pallas_call(
        pack_kernel,
        in_specs=[pl.BlockSpec(memory_space=pltpu.SMEM)] + [pl.BlockSpec(memory_space=pltpu.VMEM)] * 4,
        out_shape=jax.ShapeDtypeStruct((2320, 128), jnp.bfloat16),
    )(n, *parts)


def shift(v, axis, d):
    n = {"zh": 2, "x": 4, "c": 2, "y": 4, "zl": 2}[axis]
    return lax.ppermute(v, axis, [(i, (i + d) % n) for i in range(n)])


def scatter_sums(v):
    own, p1, p2, m1 = v[0:2], v[2:4], v[4:6], v[6:8]
    a, b = shift(p2[0], "y", 1), shift(p2[1], "y", -1)
    c, d = shift(p1[1], "y", 1), shift(m1[0], "y", -1)
    e = shift(bf16(f32(p1[0]) + f32(a)), "y", 1)
    g = shift(bf16(f32(m1[1]) + f32(b)), "y", -1)
    keep = f32(own[0]) + f32(e) + f32(d)
    away = shift(bf16(f32(own[1]) + f32(c) + f32(g)), "zl", 1)
    return keep + f32(away)


def on_device(queries, fresh_keys, fresh_values, cache_keys, cache_values, lengths, segment, weight):
    zh, x, c, y, zl = [lax.axis_index(a) for a in ("zh", "x", "c", "y", "zl")]
    rows = lambda v: v.reshape(-1, 128)
    kv = pack(lengths, rows(cache_keys), rows(fresh_keys), rows(cache_values), rows(fresh_values))
    q0 = queries.reshape(2, R, 128)
    right, left = shift(kv, "x", 1), shift(kv, "x", -1)
    qc = shift(q0, "c", 1)
    qz = shift(q0, "zh", 1)
    qzc = shift(qz, "c", 1)
    ko, vo = shift(right[:1168], "x", 1), shift(left[1168:], "x", -1)
    far = shift(weight, "c", 1)

    seg = segment.reshape(16, 128)
    rest, dxs = [(right,), (left,), (ko, vo)], (3, 1, 2)
    near = lambda q, group: attention(seg, q, group, [(kv,)], (0,), None)
    p0, pc = near(q0, (0, 0)), near(qc, (0, 1))
    qz_late, _, _ = lax.optimization_barrier((qz, right, left))
    pz, pzc = near(qz_late, (1, 0)), near(qzc, (1, 1))
    done = lambda q, group, init: attention(seg, q, group, rest, dxs, init)
    dzc = done(qzc, (1, 1), pzc)
    zc_in = shift(dzc, "c", 1)
    pz, _ = lax.optimization_barrier((pz, dzc))
    dz = done(qz, (1, 0), pz)
    chip_far = merge(dz, zc_in)
    from_z = shift(chip_far, "zh", 1)
    pc, _ = lax.optimization_barrier((pc, chip_far))
    dc = done(qc, (0, 1), pc)
    c_in = shift(dc, "c", 1)
    p0, _ = lax.optimization_barrier((p0, dc))
    d0 = done(q0, (0, 0), p0)
    att, *flats = last_merge(d0, c_in, from_z)

    slots = []
    for zz, dx in [(zh, 0), (zh, 3), (zh, 1), (zh, 2), (1 - zh, 0), (1 - zh, 3), (1 - zh, 1), (1 - zh, 2)]:
        xx = (x + dx) % 4
        slots.append(((zz * 2 + xx // 2 - y) % 4) * 2 + (xx % 2 + zl) % 2)

    arr, slots = None, jnp.stack(slots).astype(jnp.int32)
    for j, a in enumerate(flats):
        az = shift(a, "zh", 1)
        r, le = shift(a, "x", 1), shift(a, "x", -1)
        rz, lz = shift(az, "x", 1), shift(az, "x", -1)
        o = shift(le if j else r, "x", -1 if j else 1)
        oz = shift(o, "zh", 1)
        arr = assemble(slots, [a, r, le, o, az, rz, lz, oz], arr)
    arr = arr.reshape(1024, 2048)
    dot = lambda w: bf16(jnp.dot(arr, w, preferred_element_type=jnp.float32)).reshape(8, 128, 1024)
    theirs = shift(bf16(scatter_sums(dot(far))), "c", 1)
    mine = bf16(scatter_sums(dot(weight)))
    attended = att.reshape(128, 16, 128)
    mixed = jnp.where(c == 0, jnp.concatenate([mine, theirs], 0), jnp.concatenate([theirs, mine], 0))
    return attended, mixed


def solution(mesh):
    fine = Mesh(mesh.devices.reshape(2, 4, 2, 4, 2), ("zh", "x", "c", "y", "zl"))
    ctx, tp = ("zh", "x", "c"), ("y", "zl")
    heads = P(ctx, tp, None)
    return jax.shard_map(
        on_device,
        mesh=fine,
        in_specs=(heads, heads, heads, heads, heads, P(ctx), P(), P(tp, ctx)),
        out_specs=(heads, P(tp, ctx)),
        check_vma=False,
    )
```
